256 devices in a mesh: gx: 8 (over z_lo, x), gy: 4 (over y), gz: 8 (over z_hi, core).
Axes of the slice: x: 4, y: 4, z: 8 (z_hi: 4, z_lo: 2; z = z_hi * 2 + z_lo), core: 2. Of those that a mesh axis runs over, the one named last changes fastest.
Arguments:
- orbitals: float32 [96, 48, 128, 256], P('gx', 'gy', 'gz'), may hold values from -6 to 6
- potential: float32 [96, 48, 128], P('gx', 'gy', 'gz'), may hold values from -2 to 0.5
- eig_blocks: float32 [65536, 256], P(('gx', 'gy', 'gz')), may hold values from -0.375 to 0.375
- owners: int32 [2], replicated, may hold values from 0 to 255
- block_ids: int32 [2], replicated, may hold values from 0 to 7
Outputs:
- filtered: float32 [96, 48, 128, 64], P('gx', 'gy', 'gz')
The draws below stay inside these ranges and needn't reach their ends.
All inputs are finite; a program needn't handle non-finite values.
Results may differ from the reference program's by a relative error of at most 0.00012.
Values sent between devices are 32-bit elements; how exact they have to be, the bound alone decides.
A program may use at most 192 MiB of HBM per device.

```python
import jax
import jax.numpy as jnp
from jax import lax

STATES = 256
PCOL = 32
NX = 96
NY = 48
NZ = 128
OWNERS = 256


def level_of(rng, extent, split, low, top_value):
    def one(axis_at, blocks):
        draws = jax.random.uniform(jax.random.fold_in(jax.random.fold_in(rng, 6), axis_at), (blocks,), jnp.float32, low / len(split), top_value / len(split))
        return jnp.repeat(jnp.exp(draws), extent[axis_at] // blocks).reshape((-1,) + (1,) * (len(extent) - axis_at - 1))

    gain = one(*split[0])
    for cut in split[1:]:
        gain = gain * one(*cut)
    return gain


def normal_values(stream_key, extent, deviation, limit, cuts=(), dtype=jnp.bfloat16):
    gain = level_of(stream_key, extent, cuts, -0.22, 0.18) if cuts else 1.0
    result = jax.random.normal(stream_key, extent, jnp.float32) * deviation * gain
    return jnp.minimum(jnp.maximum(result, -limit), limit).astype(dtype)


def setup_inputs(seed: int = 0) -> dict:
    seeds = jax.random.split(jax.random.key(seed), 6)
    return {
        "orbitals": normal_values(seeds[0], (NX, NY, NZ, STATES), 1.0, 6.0, ((0, 8), (1, 4), (2, 8)), jnp.float32),
        "potential": jnp.clip(-2.0 + 2.5 * jax.random.uniform(seeds[1], (NX, NY, NZ), jnp.float32) ** level_of(seeds[1], (NX, NY, NZ), ((0, 8), (1, 4), (2, 8)), -0.2, 0.2), -2.0, 0.5),
        "eig_blocks": normal_values(seeds[2], (OWNERS * STATES, STATES), STATES ** -0.5, 0.375, ((0, 256),), jnp.float32),
        "owners": jax.random.randint(seeds[3], (2,), 0, OWNERS).astype(jnp.int32),
        "block_ids": jax.random.randint(seeds[4], (2,), 0, STATES // PCOL).astype(jnp.int32),
    }


coef_list = (8.0 / 5.0, -1.0 / 5.0, 8.0 / 315.0, -1.0 / 560.0)
coef_zero = -205.0 / 72.0
center = 5.5
half = 5.0


def hamiltonian(field, potential):
    lap = 3.0 * coef_zero * field
    for axis in range(3):
        for offset in range(4):
            shift = offset + 1
            lap = lap + coef_list[offset] * (jnp.roll(field, shift, axis) + jnp.roll(field, -shift, axis))
    return -0.5 * lap + potential[..., None] * field


def reference(orbitals, potential, eig_blocks, owners, block_ids):
    blocks = eig_blocks.reshape(OWNERS, STATES, STATES)
    panel_list = []
    for which in range(2):
        matrix = lax.dynamic_index_in_dim(blocks, owners[which].astype(jnp.int32), 0, keepdims=False)
        start = (block_ids[which] * PCOL).astype(jnp.int32)
        panel_list.append(lax.dynamic_slice_in_dim(matrix, start, PCOL, 1))
    rotation = jnp.concatenate(panel_list, axis=1)
    psi = jnp.dot(orbitals.reshape(-1, STATES), rotation, precision=lax.Precision.HIGHEST,
                  preferred_element_type=jnp.float32).reshape(NX, NY, NZ, 2 * PCOL)
    first = (hamiltonian(psi, potential) - center * psi) / half
    second = 2.0 * (hamiltonian(first, potential) - center * first) / half - psi
    return 2.0 * (hamiltonian(second, potential) - center * second) / half - first
```

```python
import jax
import jax.numpy as jnp
from jax import lax
from jax.experimental import pallas as pl
from jax.experimental.pallas import tpu as pltpu
from jax.sharding import PartitionSpec as P

MESH = pl.DeviceIdType.MESH
PCOL = 32
coef_list = (8.0 / 5.0, -1.0 / 5.0, 8.0 / 315.0, -1.0 / 560.0)
coef_zero = -205.0 / 72.0
center = 5.5
half = 5.0
SLABS = (0, 8, 4)


def kernel(own_ref, bid_ref, orb_ref, pot_ref, eig_ref, out_ref,
           orb, eig, contrib, r1, r2, full, e0, e1, e2, diag, zs, zr, ohi, olo, w,
           load_sem, g_send, g_recv, h_send, h_recv):
    gx, gy, gz = lax.axis_index("gx"), lax.axis_index("gy"), lax.axis_index("gz")
    x = lax.rem(gx, 4)
    zlo = lax.div(gx, 4)
    fields = (e0, e1, e2)

    plane = []
    line = []
    for k in range(1, 16):
        px, py = lax.rem(x + k // 4, 4), lax.rem(gy + k % 4, 4)
        plane.append((k, px * 4 + py, (zlo * 4 + px, py, gz)))
        pz, pc = lax.rem(zlo + k // 8, 2), lax.rem(gz + k % 8, 8)
        line.append((k, (pz * 4 + x, gy, pc)))
    me = x * 4 + gy
    xup, xdown = (lax.rem(gx + 1, 8), gy, gz), (lax.rem(gx + 7, 8), gy, gz)
    yup, ydown = (gx, lax.rem(gy + 1, 4), gz), (gx, lax.rem(gy + 3, 4), gz)
    zup, zdown = (gx, gy, lax.rem(gz + 1, 8)), (gx, gy, lax.rem(gz + 7, 8))

    barrier = pltpu.get_barrier_semaphore()
    peers = [p for _, _, p in plane] + [p for _, p in line] + [xup, xdown]
    for p in peers:
        pl.semaphore_signal(barrier, inc=1, device_id=p, device_id_type=MESH)

    load_eig = pltpu.make_async_copy(eig_ref, eig, load_sem.at[0])
    load_eig.start()
    load_orb = pltpu.make_async_copy(orb_ref, orb, load_sem.at[1])
    load_orb.start()

    load_eig.wait()
    my_id = (gx * 4 + gy) * 8 + gz
    lane = lax.broadcasted_iota(jnp.int32, (256, 128), 1)
    row = lax.broadcasted_iota(jnp.int32, (256, 128), 0)
    state = lax.rem(lane, 64)
    first = state < PCOL
    owner = jnp.where(first, own_ref[0], own_ref[1])
    column = jnp.where(first, bid_ref[0], bid_ref[1]) * PCOL + lax.rem(state, PCOL)
    pick = jnp.where((row == column) & (owner == my_id), 1.0, 0.0)
    top = jnp.dot(eig[0:128], jnp.where(lane < 64, pick, 0.0), precision=lax.Precision.HIGHEST,
                  preferred_element_type=jnp.float32)
    low = jnp.dot(eig[128:256], jnp.where(lane < 64, 0.0, pick), precision=lax.Precision.HIGHEST,
                  preferred_element_type=jnp.float32)
    contrib[...] = (top + low).reshape(16, 8, 128)
    r1[0] = contrib[me]

    pl.semaphore_wait(barrier, len(peers))

    for k, j, dev in plane:
        pltpu.make_async_remote_copy(src_ref=contrib.at[j], dst_ref=r1.at[k], send_sem=g_send.at[0], recv_sem=g_recv.at[0],
                                     device_id=dev, device_id_type=MESH).start()

    load_orb.wait()

    def split(i, carry):
        for zh in range(2):
            o = orb[i, :, pl.ds(8 * zh, 8), :].reshape(96, 256)
            hi = o.astype(jnp.bfloat16)
            rows = pl.ds(pl.multiple_of(i * 96, 96), 96)
            ohi[zh, rows, :] = hi
            olo[zh, rows, :] = (o - hi.astype(jnp.float32)).astype(jnp.bfloat16)
        return carry

    lax.fori_loop(0, 12, split, 0)

    zmask = lax.broadcasted_iota(jnp.int32, (12, 8, 16), 1) == lax.rem(lax.broadcasted_iota(jnp.int32, (12, 8, 16), 2), 8)
    spread = jnp.where(lax.div(lax.broadcasted_iota(jnp.int32, (16, 128), 0), 8)
                       == lax.div(lax.broadcasted_iota(jnp.int32, (16, 128), 1), 64), 1.0, 0.0)

    def diagonal(i, carry):
        v = (pot_ref[i] - center) / half - 0.3 * coef_zero
        a = jnp.where(zmask, jnp.broadcast_to(v[:, None, :], (12, 8, 16)), 0.0).reshape(96, 16)
        diag[i] = jnp.dot(a, spread, precision=lax.Precision.HIGHEST,
                          preferred_element_type=jnp.float32).reshape(12, 8, 128)
        return carry

    lax.fori_loop(0, 12, diagonal, 0)

    def all_arrived(n, buf):
        return pltpu.make_async_remote_copy(src_ref=buf.at[pl.ds(1, 15)], dst_ref=buf.at[pl.ds(1, 15)], send_sem=g_send.at[n],
                                            recv_sem=g_recv.at[n], device_id=xup, device_id_type=MESH)

    all_arrived(0, r1).wait_recv()
    r2[0] = jnp.sum(r1[...], axis=0)
    for k, dev in line:
        pltpu.make_async_remote_copy(src_ref=r2.at[0], dst_ref=r2.at[k], send_sem=g_send.at[1], recv_sem=g_recv.at[1],
                                     device_id=dev, device_id_type=MESH).start()
    all_arrived(1, r2).wait_recv()
    full[me] = jnp.sum(r2[...], axis=0)
    for k, j, dev in plane:
        pltpu.make_async_remote_copy(src_ref=full.at[me], dst_ref=full.at[me], send_sem=g_send.at[2], recv_sem=g_recv.at[2],
                                     device_id=dev, device_id_type=MESH).start()
    all_arrived(2, full).wait_recv()

    rot = full[...].reshape(128, 128)
    swapped = pltpu.roll(rot, 64, 1)
    lane = lax.broadcasted_iota(jnp.int32, (128, 128), 1)
    for zh in range(2):
        keep = (lane < 64) if zh == 0 else (lane >= 64)
        for kh in range(2):
            part = jnp.where(keep, rot if zh == kh else swapped, 0.0)
            hi = part.astype(jnp.bfloat16)
            w[zh, pl.ds(128 * kh, 128), 0:128] = hi
            w[zh, pl.ds(128 * kh, 128), 128:256] = (part - hi.astype(jnp.float32)).astype(jnp.bfloat16)

    sub = lax.broadcasted_iota(jnp.int32, (8, 128), 0)
    cross = (sub < 4) == (lax.broadcasted_iota(jnp.int32, (8, 128), 1) >= 64)

    def halo(stage, slab=None):
        e = fields[stage]
        out = []

        def add(n, src, dst, dev):
            out.append(pltpu.make_async_remote_copy(src_ref=src, dst_ref=dst, send_sem=h_send.at[stage, n],
                                                    recv_sem=h_recv.at[stage, n], device_id=dev, device_id_type=MESH))

        inner = pl.ds(4, 12)
        for s, x0 in enumerate(SLABS):
            if slab is not None and s != slab:
                continue
            if x0 == 8:
                add(0, e.at[pl.ds(12, 4), inner], e.at[pl.ds(0, 4), inner], xup)
            if x0 == 0:
                add(1, e.at[pl.ds(4, 4), inner], e.at[pl.ds(16, 4), inner], xdown)
            layers = pl.ds(x0, 4)
            add(2 + s, zs.at[stage, layers, :, pl.ds(4, 4)], zr.at[stage, layers, :, pl.ds(4, 4)], zup)
            add(5 + s, zs.at[stage, layers, :, pl.ds(0, 4)], zr.at[stage, layers, :, pl.ds(0, 4)], zdown)
            layers = pl.ds(x0 + 4, 4)
            add(8 + s, e.at[layers, pl.ds(12, 4)], e.at[layers, pl.ds(0, 4)], yup)
            add(11 + s, e.at[layers, pl.ds(4, 4)], e.at[layers, pl.ds(16, 4)], ydown)
        return out

    def pack(stage, i, values):
        for y in range(6):
            zs[stage, i, y] = jnp.where(cross, pltpu.roll(values[y], 64, 1), values[y + 6])

    for s, x0 in enumerate(SLABS):
        rows = pl.ds(x0 * 96, 384)
        acc = jnp.dot(ohi[0, rows, :], w[0], preferred_element_type=jnp.float32)
        acc = acc + jnp.dot(ohi[1, rows, :], w[1], preferred_element_type=jnp.float32)
        psi = acc[:, 0:128] + acc[:, 128:256]
        psi = psi + jnp.dot(olo[0, rows, :], w[0, :, 0:128], preferred_element_type=jnp.float32)
        psi = psi + jnp.dot(olo[1, rows, :], w[1, :, 0:128], preferred_element_type=jnp.float32)
        e0[pl.ds(4 + x0, 4), pl.ds(4, 12)] = psi.reshape(4, 12, 8, 128)

        def pack_layer(i, carry):
            pack(0, i, [e0[i + 4, y + 4] for y in range(12)])
            return carry

        lax.fori_loop(x0, x0 + 4, pack_layer, 0)
        for cp in halo(0, s):
            cp.start()

    for stage in range(3):
        e = fields[stage]
        factor = 1.0 if stage == 0 else 2.0
        weights = [-0.1 * factor * c for c in coef_list]
        for cp in halo(stage):
            cp.wait_recv()

        def layer(i, carry):
            values = []
            column = [e[i + 4, y] for y in range(20)]
            for y in range(12):
                c = column[y + 4]
                rolled = pltpu.roll(c, 64, 1)
                beyond = zr[stage, i, y % 6]
                if y >= 6:
                    beyond = pltpu.roll(beyond, 64, 1)
                beyond = jnp.where(cross, beyond, rolled)
                total = factor * diag[i, y] * c
                for m in range(1, 5):
                    up = pltpu.roll(jnp.where(sub < m, beyond, c), 8 - m, 0)
                    down = pltpu.roll(jnp.where(sub >= 8 - m, beyond, c), m, 0)
                    near = (up + down) + (column[y + 4 + m] + column[y + 4 - m]) + (e[i + 4 + m, y + 4] + e[i + 4 - m, y + 4])
                    total = total + weights[m - 1] * near
                if stage > 0:
                    total = total - fields[stage - 1][i + 4, y + 4]
                if stage < 2:
                    fields[stage + 1][i + 4, y + 4] = total
                    values.append(total)
                else:
                    out_ref[i, y, 0:8, :] = total[:, 0:64]
                    out_ref[i, y, 8:16, :] = pltpu.roll(total, 64, 1)[:, 0:64]
            if stage < 2:
                pack(stage + 1, i, values)
            return carry

        for s, x0 in enumerate(SLABS):
            lax.fori_loop(x0, x0 + 4, layer, 0)
            if stage < 2:
                for cp in halo(stage + 1, s):
                    cp.start()

    for n, buf in enumerate((r1, r2, full)):
        all_arrived(n, buf).wait_send()
    for stage in range(3):
        for cp in halo(stage):
            cp.wait_send()


def per_device(orbitals, potential, eig_blocks, owners, block_ids):
    smem = pl.BlockSpec(memory_space=pltpu.SMEM)
    vmem = pl.BlockSpec(memory_space=pltpu.VMEM)
    hbm = pl.BlockSpec(memory_space=pl.ANY)
    f32, bf16 = jnp.float32, jnp.bfloat16
    scratch = [
        pltpu.VMEM((12, 12, 16, 256), f32),
        pltpu.VMEM((256, 256), f32),
        pltpu.VMEM((16, 8, 128), f32),
        pltpu.VMEM((16, 8, 128), f32),
        pltpu.VMEM((16, 8, 128), f32),
        pltpu.VMEM((16, 8, 128), f32),
        pltpu.VMEM((20, 20, 8, 128), f32),
        pltpu.VMEM((20, 20, 8, 128), f32),
        pltpu.VMEM((20, 20, 8, 128), f32),
        pltpu.VMEM((12, 12, 8, 128), f32),
        pltpu.VMEM((3, 12, 6, 8, 128), f32),
        pltpu.VMEM((3, 12, 6, 8, 128), f32),
        pltpu.VMEM((2, 1152, 256), bf16),
        pltpu.VMEM((2, 1152, 256), bf16),
        pltpu.VMEM((2, 256, 256), bf16),
        pltpu.SemaphoreType.DMA((2,)),
        pltpu.SemaphoreType.DMA((3,)),
        pltpu.SemaphoreType.DMA((3,)),
        pltpu.SemaphoreType.DMA((3, 14)),
        pltpu.SemaphoreType.DMA((3, 14)),
    ]
    return pl.pallas_call(
        kernel,
        out_shape=jax.ShapeDtypeStruct((12, 12, 16, 64), f32),
        in_specs=[smem, smem, hbm, vmem, hbm],
        out_specs=vmem,
        scratch_shapes=scratch,
        compiler_params=pltpu.CompilerParams(
            collective_id=0, has_side_effects=True, vmem_limit_bytes=56 * 2**20
        ),
        name="rotate_filter",
    )(owners, block_ids, orbitals, potential, eig_blocks)


def solution(mesh):
    placed = (P("gx", "gy", "gz", None), P("gx", "gy", "gz"), P(("gx", "gy", "gz"), None), P(), P())
    return jax.shard_map(
        per_device, mesh=mesh, in_specs=placed, out_specs=P("gx", "gy", "gz", None), check_vma=False
    )
```

```python
import jax
import jax.numpy as jnp
from jax import lax
from jax.experimental import pallas as pl
from jax.experimental.pallas import tpu as pltpu
from jax.sharding import PartitionSpec as P

MESH = pl.DeviceIdType.MESH
PCOL = 32
coef_list = (8.0 / 5.0, -1.0 / 5.0, 8.0 / 315.0, -1.0 / 560.0)
coef_zero = -205.0 / 72.0
center = 5.5
half = 5.0


def kernel(own_hbm, bid_hbm, orb_ref, pot_hbm, eig_ref, out_ref,
           own_ref, bid_ref, pot_ref, orb, eig, contrib, r1, r2, full, e, diag, xs, xr, zs, zr, done, ohi, olo, w,
           load_sem, g_send, g_recv, h_send, h_recv):
    gx, gy, gz = lax.axis_index("gx"), lax.axis_index("gy"), lax.axis_index("gz")
    x = lax.rem(gx, 4)
    zlo = lax.div(gx, 4)

    loads = []
    for n, (src, dst) in enumerate(((own_hbm, own_ref), (bid_hbm, bid_ref), (eig_ref, eig), (orb_ref, orb), (pot_hbm, pot_ref))):
        loads.append(pltpu.make_async_copy(src, dst, load_sem.at[n]))
        loads[n].start()

    plane = []
    line = []
    for k in range(1, 16):
        px, py = lax.rem(x + k // 4, 4), lax.rem(gy + k % 4, 4)
        plane.append((k, px * 4 + py, (zlo * 4 + px, py, gz)))
        pz, pc = lax.rem(zlo + k // 8, 2), lax.rem(gz + k % 8, 8)
        line.append((k, (pz * 4 + x, gy, pc)))
    me = x * 4 + gy
    xup, xdown = (lax.rem(gx + 1, 8), gy, gz), (lax.rem(gx + 7, 8), gy, gz)
    yup, ydown = (gx, lax.rem(gy + 1, 4), gz), (gx, lax.rem(gy + 3, 4), gz)
    zup, zdown = (gx, gy, lax.rem(gz + 1, 8)), (gx, gy, lax.rem(gz + 7, 8))

    barrier = pltpu.get_barrier_semaphore()
    peers = [p for _, _, p in plane] + [p for _, p in line] + [xup, xdown]
    for p in peers:
        pl.semaphore_signal(barrier, inc=1, device_id=p, device_id_type=MESH)

    for n in range(3):
        loads[n].wait()
    my_id = (gx * 4 + gy) * 8 + gz
    lane = lax.broadcasted_iota(jnp.int32, (256, 128), 1)
    row = lax.broadcasted_iota(jnp.int32, (256, 128), 0)
    state = lax.rem(lane, 64)
    first = state < PCOL
    owner = jnp.where(first, own_ref[0], own_ref[1])
    column = jnp.where(first, bid_ref[0], bid_ref[1]) * PCOL + lax.rem(state, PCOL)
    pick = jnp.where((row == column) & (owner == my_id), 1.0, 0.0)
    top = jnp.dot(eig[0:128], jnp.where(lane < 64, pick, 0.0), precision=lax.Precision.HIGHEST,
                  preferred_element_type=jnp.float32)
    low = jnp.dot(eig[128:256], jnp.where(lane < 64, 0.0, pick), precision=lax.Precision.HIGHEST,
                  preferred_element_type=jnp.float32)
    contrib[...] = (top + low).reshape(16, 8, 128)
    r1[0] = contrib[me]

    pl.semaphore_wait(barrier, len(peers))

    for k, j, dev in plane:
        pltpu.make_async_remote_copy(src_ref=contrib.at[j], dst_ref=r1.at[k], send_sem=g_send.at[0], recv_sem=g_recv.at[0],
                                     device_id=dev, device_id_type=MESH).start()

    loads[3].wait()

    def split(i, carry):
        rows = pl.ds(pl.multiple_of(i * 96, 96), 96)
        for zh in range(2):
            for xh in range(2):
                o = orb[i + 6 * xh, :, pl.ds(8 * zh, 8), :].reshape(96, 256)
                hi = o.astype(jnp.bfloat16)
                columns = pl.ds(256 * (2 * zh + xh), 256)
                ohi[rows, columns] = hi
                olo[rows, columns] = (o - hi.astype(jnp.float32)).astype(jnp.bfloat16)
        return carry

    lax.fori_loop(0, 6, split, 0)

    loads[4].wait()
    zmask = lax.broadcasted_iota(jnp.int32, (12, 8, 16), 1) == lax.rem(lax.broadcasted_iota(jnp.int32, (12, 8, 16), 2), 8)
    zhalf = lax.div(lax.broadcasted_iota(jnp.int32, (16, 128), 0), 8)
    quarter = lax.div(lax.broadcasted_iota(jnp.int32, (16, 128), 1), 32)

    def diagonal(i, carry):
        total = 0.0
        for xh in range(2):
            v = (pot_ref[i + 6 * xh] - center) / half - 0.3 * coef_zero
            a = jnp.where(zmask, jnp.broadcast_to(v[:, None, :], (12, 8, 16)), 0.0).reshape(96, 16)
            spread = jnp.where(quarter == 2 * zhalf + xh, 1.0, 0.0)
            total = total + jnp.dot(a, spread, precision=lax.Precision.HIGHEST, preferred_element_type=jnp.float32)
        diag[i] = total.reshape(12, 8, 128)
        return carry

    lax.fori_loop(0, 6, diagonal, 0)

    def all_arrived(n, buf):
        return pltpu.make_async_remote_copy(src_ref=buf.at[pl.ds(1, 15)], dst_ref=buf.at[pl.ds(1, 15)], send_sem=g_send.at[n],
                                            recv_sem=g_recv.at[n], device_id=xup, device_id_type=MESH)

    all_arrived(0, r1).wait_recv()
    r2[0] = jnp.sum(r1[...], axis=0)
    for k, dev in line:
        pltpu.make_async_remote_copy(src_ref=r2.at[0], dst_ref=r2.at[k], send_sem=g_send.at[1], recv_sem=g_recv.at[1],
                                     device_id=dev, device_id_type=MESH).start()
    all_arrived(1, r2).wait_recv()
    full[me] = jnp.sum(r2[...], axis=0)
    for k, j, dev in plane:
        pltpu.make_async_remote_copy(src_ref=full.at[me], dst_ref=full.at[me], send_sem=g_send.at[2], recv_sem=g_recv.at[2],
                                     device_id=dev, device_id_type=MESH).start()
    all_arrived(2, full).wait_recv()

    sub = lax.broadcasted_iota(jnp.int32, (8, 128), 0)
    lane = lax.broadcasted_iota(jnp.int32, (8, 128), 1)
    cross = (sub < 4) == (lane >= 64)
    lower = lax.rem(lane, 64) < 32
    wide = lax.div(lax.broadcasted_iota(jnp.int32, (128, 128), 1), 32)

    def weights(g):
        rot = full[...].reshape(128, 128)
        rolled = [rot] + [pltpu.roll(rot, 32 * r, 1) for r in range(1, 4)]
        for b in range(4):
            for kh in range(2):
                part = jnp.where(wide == b, rolled[(b - 2 * kh - g) % 4], 0.0)
                hi = part.astype(jnp.bfloat16)
                rows = pl.ds(256 * b + 128 * kh, 128)
                w[g, rows, 0:128] = hi
                w[g, rows, 128:256] = (part - hi.astype(jnp.float32)).astype(jnp.bfloat16)

    def halo(k, g):
        inner = pl.ds(4, 6)
        field = e.at[k, g]
        pairs = (
            (xs.at[k, g, 0], xr.at[k, g, 0], xup),
            (xs.at[k, g, 1], xr.at[k, g, 1], xdown),
            (zs.at[k, g, :, :, pl.ds(4, 4)], zr.at[k, g, :, :, pl.ds(4, 4)], zup),
            (zs.at[k, g, :, :, pl.ds(0, 4)], zr.at[k, g, :, :, pl.ds(0, 4)], zdown),
            (field.at[inner, pl.ds(12, 4)], field.at[inner, pl.ds(0, 4)], yup),
            (field.at[inner, pl.ds(4, 4)], field.at[inner, pl.ds(16, 4)], ydown),
        )
        return [
            pltpu.make_async_remote_copy(src_ref=src, dst_ref=dst, send_sem=h_send.at[k, g, n], recv_sem=h_recv.at[k, g, n],
                                         device_id=dev, device_id_type=MESH)
            for n, (src, dst, dev) in enumerate(pairs)
        ]

    def send(k, g):
        field = e.at[k, g]

        def pack(y, carry):
            for at, side in ((y, 0), (y + 6, 1)):
                c = [field[4 + i, 4 + at] for i in range(6)]
                up = [pltpu.roll(c[i], 32, 1) for i in range(2, 6)]
                down = [pltpu.roll(c[i], 96, 1) for i in range(4)]
                for j in range(2):
                    xs[k, g, 0, j, at] = jnp.where(lower, down[2 + j], c[4 + j])
                    xs[k, g, 1, j, at] = jnp.where(lower, c[j], up[j])
                for i in range(4):
                    field[i, 4 + at] = up[i]
                    field[10 + i, 4 + at] = down[i]
                if side == 0:
                    kept = c
            for i in range(6):
                zs[k, g, i, y] = jnp.where(cross, pltpu.roll(kept[i], 64, 1), c[i])
            return carry

        copies = halo(k, g)
        lax.fori_loop(0, 6, pack, 0, unroll=6)
        for cp in copies:
            cp.start()

    def receive(k, g):
        field = e.at[k, g]
        for cp in halo(k, g):
            cp.wait_recv()

        def unpack(y, carry):
            for j in range(2):
                before, after = xr[k, g, 0, j, y], xr[k, g, 1, j, y]
                field[j, 4 + y] = jnp.where(lower, before, field[j, 4 + y])
                field[2 + j, 4 + y] = jnp.where(lower, pltpu.roll(before, 96, 1), field[2 + j, 4 + y])
                field[10 + j, 4 + y] = jnp.where(lower, field[10 + j, 4 + y], pltpu.roll(after, 32, 1))
                field[12 + j, 4 + y] = jnp.where(lower, field[12 + j, 4 + y], after)
            return carry

        lax.fori_loop(0, 12, unpack, 0, unroll=12)

    def stencil(k, g):
        factor = 1.0 if k == 0 else 2.0
        factors = [-0.1 * factor * c for c in coef_list]
        field = e.at[k, g]

        def layer(i, carry):
            column = [field[i + 4, y] for y in range(20)]
            for y in range(12):
                c = column[y + 4]
                beyond = zr[k, g, i, y % 6]
                if y >= 6:
                    beyond = pltpu.roll(beyond, 64, 1)
                beyond = jnp.where(cross, beyond, pltpu.roll(c, 64, 1))
                total = factor * diag[i, y] * c
                for m in range(1, 5):
                    up = pltpu.roll(jnp.where(sub < m, beyond, c), 8 - m, 0)
                    down = pltpu.roll(jnp.where(sub >= 8 - m, beyond, c), m, 0)
                    near = ((up + down) + (column[y + 4 + m] + column[y + 4 - m])
                            + (field[i + 4 + m, y + 4] + field[i + 4 - m, y + 4]))
                    total = total + factors[m - 1] * near
                if k > 0:
                    total = total - e[k - 1, g, i + 4, y + 4]
                if k < 2:
                    e[k + 1, g, i + 4, y + 4] = total
                elif g == 0:
                    done[i, y] = total
                else:
                    even = jnp.where(lower, done[i, y], pltpu.roll(total, 32, 1))
                    odd = jnp.where(lower, pltpu.roll(done[i, y], 96, 1), total)
                    for xh, v in enumerate((even, odd)):
                        out_ref[i + 6 * xh, y, 0:8, :] = v[:, 0:64]
                        out_ref[i + 6 * xh, y, 8:16, :] = pltpu.roll(v, 64, 1)[:, 0:64]
            return carry

        lax.fori_loop(0, 6, layer, 0, unroll=2)

    for g in range(2):
        weights(g)
        acc = jnp.dot(ohi[...], w[g], preferred_element_type=jnp.float32)
        acc = acc + jnp.dot(olo[...], w[g], preferred_element_type=jnp.float32)
        e[0, g, pl.ds(4, 6), pl.ds(4, 12)] = (acc[:, 0:128] + acc[:, 128:256]).reshape(6, 12, 8, 128)
        send(0, g)

    for k in range(3):
        for g in range(2):
            receive(k, g)
            stencil(k, g)
            if k < 2:
                send(k + 1, g)

    for n, buf in enumerate((r1, r2, full)):
        all_arrived(n, buf).wait_send()
    for k in range(3):
        for g in range(2):
            for cp in halo(k, g):
                cp.wait_send()


def per_device(orbitals, potential, eig_blocks, owners, block_ids):
    hbm = pl.BlockSpec(memory_space=pl.ANY)
    f32, bf16 = jnp.float32, jnp.bfloat16
    scratch = [
        pltpu.SMEM((2,), jnp.int32),
        pltpu.SMEM((2,), jnp.int32),
        pltpu.VMEM((12, 12, 16), f32),
        pltpu.VMEM((12, 12, 16, 256), f32),
        pltpu.VMEM((256, 256), f32),
        pltpu.VMEM((16, 8, 128), f32),
        pltpu.VMEM((16, 8, 128), f32),
        pltpu.VMEM((16, 8, 128), f32),
        pltpu.VMEM((16, 8, 128), f32),
        pltpu.VMEM((3, 2, 14, 20, 8, 128), f32),
        pltpu.VMEM((6, 12, 8, 128), f32),
        pltpu.VMEM((3, 2, 2, 2, 12, 8, 128), f32),
        pltpu.VMEM((3, 2, 2, 2, 12, 8, 128), f32),
        pltpu.VMEM((3, 2, 6, 6, 8, 128), f32),
        pltpu.VMEM((3, 2, 6, 6, 8, 128), f32),
        pltpu.VMEM((6, 12, 8, 128), f32),
        pltpu.VMEM((576, 1024), bf16),
        pltpu.VMEM((576, 1024), bf16),
        pltpu.VMEM((2, 1024, 256), bf16),
        pltpu.SemaphoreType.DMA((5,)),
        pltpu.SemaphoreType.DMA((3,)),
        pltpu.SemaphoreType.DMA((3,)),
        pltpu.SemaphoreType.DMA((3, 2, 6)),
        pltpu.SemaphoreType.DMA((3, 2, 6)),
    ]
    return pl.pallas_call(
        kernel,
        out_shape=pltpu.VMEM((12, 12, 16, 64), f32),
        in_specs=[hbm] * 5,
        out_specs=pl.BlockSpec(memory_space=pltpu.VMEM),
        scratch_shapes=scratch,
        compiler_params=pltpu.CompilerParams(
            collective_id=0, has_side_effects=True, vmem_limit_bytes=56 * 2**20
        ),
        name="rotate_filter",
    )(owners, block_ids, orbitals, potential, eig_blocks)


def solution(mesh):
    placed = (P("gx", "gy", "gz", None), P("gx", "gy", "gz"), P(("gx", "gy", "gz"), None), P(), P())
    return jax.shard_map(
        per_device, mesh=mesh, in_specs=placed, out_specs=P("gx", "gy", "gz", None), check_vma=False
    )
```

```python
import jax
import jax.numpy as jnp
from jax import lax
from jax.experimental import pallas as pl
from jax.experimental.pallas import tpu as pltpu
from jax.sharding import PartitionSpec as P

MESH = pl.DeviceIdType.MESH
PCOL = 32
coef_list = (8.0 / 5.0, -1.0 / 5.0, 8.0 / 315.0, -1.0 / 560.0)
coef_zero = -205.0 / 72.0
center = 5.5
half = 5.0


def kernel(own_hbm, bid_hbm, orb_ref, pot_hbm, eig_ref, out_ref,
           own_ref, bid_ref, pot_ref, orb, eig, contrib, r1, r2, full, e, diag, xs, xr, zs, zr, done, ohi, olo, w,
           load_sem, g_send, g_recv, h_send, h_recv):
    gx, gy, gz = lax.axis_index("gx"), lax.axis_index("gy"), lax.axis_index("gz")
    x = lax.rem(gx, 4)
    zlo = lax.div(gx, 4)

    loads = []
    for n, (src, dst) in enumerate(((own_hbm, own_ref), (bid_hbm, bid_ref), (eig_ref, eig), (orb_ref, orb), (pot_hbm, pot_ref))):
        loads.append(pltpu.make_async_copy(src, dst, load_sem.at[n]))
        loads[n].start()

    plane = []
    line = []
    for k in sorted(range(1, 16), key=lambda k: -min(k // 4, 4 - k // 4) - min(k % 4, 4 - k % 4)):
        px, py = lax.rem(x + k // 4, 4), lax.rem(gy + k % 4, 4)
        plane.append((k, px * 4 + py, (zlo * 4 + px, py, gz)))
    for k in sorted(range(1, 16), key=lambda k: -min(k % 8, 8 - k % 8)):
        pz, pc = lax.rem(zlo + k // 8, 2), lax.rem(gz + k % 8, 8)
        line.append((k, (pz * 4 + x, gy, pc)))
    me = x * 4 + gy
    xup, xdown = (lax.rem(gx + 1, 8), gy, gz), (lax.rem(gx + 7, 8), gy, gz)
    yup, ydown = (gx, lax.rem(gy + 1, 4), gz), (gx, lax.rem(gy + 3, 4), gz)
    zup, zdown = (gx, gy, lax.rem(gz + 1, 8)), (gx, gy, lax.rem(gz + 7, 8))

    barrier = pltpu.get_barrier_semaphore()
    peers = [p for _, _, p in plane] + [p for _, p in line]
    for p in peers:
        pl.semaphore_signal(barrier, inc=1, device_id=p, device_id_type=MESH)

    for n in range(3):
        loads[n].wait()
    my_id = (gx * 4 + gy) * 8 + gz
    lane = lax.broadcasted_iota(jnp.int32, (256, 128), 1)
    row = lax.broadcasted_iota(jnp.int32, (256, 128), 0)
    state = lax.rem(lane, 64)
    first = state < PCOL
    owner = jnp.where(first, own_ref[0], own_ref[1])
    column = jnp.where(first, bid_ref[0], bid_ref[1]) * PCOL + lax.rem(state, PCOL)
    pick = jnp.where((row == column) & (owner == my_id), 1.0, 0.0)
    top = jnp.dot(eig[0:128], jnp.where(lane < 64, pick, 0.0), precision=lax.Precision.HIGHEST,
                  preferred_element_type=jnp.float32)
    low = jnp.dot(eig[128:256], jnp.where(lane < 64, 0.0, pick), precision=lax.Precision.HIGHEST,
                  preferred_element_type=jnp.float32)
    contrib[...] = (top + low).reshape(16, 8, 128)
    r1[0] = contrib[me]

    pl.semaphore_wait(barrier, len(peers))

    for k, j, dev in plane:
        pltpu.make_async_remote_copy(src_ref=contrib.at[j], dst_ref=r1.at[k], send_sem=g_send.at[0], recv_sem=g_recv.at[0],
                                     device_id=dev, device_id_type=MESH).start()

    def all_arrived(n, buf):
        return pltpu.make_async_remote_copy(src_ref=buf.at[pl.ds(1, 15)], dst_ref=buf.at[pl.ds(1, 15)], send_sem=g_send.at[n],
                                            recv_sem=g_recv.at[n], device_id=xup, device_id_type=MESH)

    all_arrived(0, r1).wait_recv()
    r2[0] = jnp.sum(r1[...], axis=0)
    for k, dev in line:
        pltpu.make_async_remote_copy(src_ref=r2.at[0], dst_ref=r2.at[k], send_sem=g_send.at[1], recv_sem=g_recv.at[1],
                                     device_id=dev, device_id_type=MESH).start()
    loads[3].wait()

    def split(i, carry):
        rows = pl.ds(pl.multiple_of(i * 96, 96), 96)
        for zh in range(2):
            for xh in range(2):
                o = orb[i + 6 * xh, :, pl.ds(8 * zh, 8), :].reshape(96, 256)
                hi = o.astype(jnp.bfloat16)
                columns = pl.ds(256 * (2 * zh + xh), 256)
                ohi[rows, columns] = hi
                olo[rows, columns] = (o - hi.astype(jnp.float32)).astype(jnp.bfloat16)
        return carry

    lax.fori_loop(0, 6, split, 0)

    all_arrived(1, r2).wait_recv()
    full[me] = jnp.sum(r2[...], axis=0)
    for k, j, dev in plane:
        pltpu.make_async_remote_copy(src_ref=full.at[me], dst_ref=full.at[me], send_sem=g_send.at[2], recv_sem=g_recv.at[2],
                                     device_id=dev, device_id_type=MESH).start()
    loads[4].wait()
    zmask = lax.broadcasted_iota(jnp.int32, (12, 8, 16), 1) == lax.rem(lax.broadcasted_iota(jnp.int32, (12, 8, 16), 2), 8)
    zhalf = lax.div(lax.broadcasted_iota(jnp.int32, (16, 128), 0), 8)
    quarter = lax.div(lax.broadcasted_iota(jnp.int32, (16, 128), 1), 32)

    def diagonal(i, carry):
        total = 0.0
        for xh in range(2):
            v = (pot_ref[i + 6 * xh] - center) / half - 0.3 * coef_zero
            a = jnp.where(zmask, jnp.broadcast_to(v[:, None, :], (12, 8, 16)), 0.0).reshape(96, 16)
            spread = jnp.where(quarter == 2 * zhalf + xh, 1.0, 0.0)
            total = total + jnp.dot(a, spread, precision=lax.Precision.HIGHEST, preferred_element_type=jnp.float32)
        diag[i] = total.reshape(12, 8, 128)
        return carry

    lax.fori_loop(0, 6, diagonal, 0)

    all_arrived(2, full).wait_recv()

    sub = lax.broadcasted_iota(jnp.int32, (8, 128), 0)
    lane = lax.broadcasted_iota(jnp.int32, (8, 128), 1)
    cross = (sub < 4) == (lane >= 64)
    lower = lax.rem(lane, 64) < 32
    wide = lax.div(lax.broadcasted_iota(jnp.int32, (128, 128), 1), 32)

    def weights(g):
        rot = full[...].reshape(128, 128)
        rolled = [rot] + [pltpu.roll(rot, 32 * r, 1) for r in range(1, 4)]
        for b in range(4):
            for kh in range(2):
                part = jnp.where(wide == b, rolled[(b - 2 * kh - g) % 4], 0.0)
                hi = part.astype(jnp.bfloat16)
                rows = pl.ds(256 * b + 128 * kh, 128)
                w[g, rows, 0:128] = hi
                w[g, rows, 128:256] = (part - hi.astype(jnp.float32)).astype(jnp.bfloat16)

    def halo(k, g):
        inner = pl.ds(4, 6)
        field = e.at[k, g]
        pairs = (
            (zs.at[k, g, :, :, pl.ds(4, 4)], zr.at[k, g, :, :, pl.ds(4, 4)], zup),
            (zs.at[k, g, :, :, pl.ds(0, 4)], zr.at[k, g, :, :, pl.ds(0, 4)], zdown),
            (xs.at[k, g, 0], xr.at[k, g, 0], xup),
            (xs.at[k, g, 1], xr.at[k, g, 1], xdown),
            (field.at[inner, pl.ds(12, 4)], field.at[inner, pl.ds(0, 4)], yup),
            (field.at[inner, pl.ds(4, 4)], field.at[inner, pl.ds(16, 4)], ydown),
        )
        return [
            pltpu.make_async_remote_copy(src_ref=src, dst_ref=dst, send_sem=h_send.at[k, g, n], recv_sem=h_recv.at[k, g, n],
                                         device_id=dev, device_id_type=MESH)
            for n, (src, dst, dev) in enumerate(pairs)
        ]

    def send(k, g):
        field = e.at[k, g]

        def pack(y, carry):
            for at, side in ((y, 0), (y + 6, 1)):
                c = [field[4 + i, 4 + at] for i in range(6)]
                up = [pltpu.roll(c[i], 32, 1) for i in range(2, 6)]
                down = [pltpu.roll(c[i], 96, 1) for i in range(4)]
                for j in range(2):
                    xs[k, g, 0, j, at] = jnp.where(lower, down[2 + j], c[4 + j])
                    xs[k, g, 1, j, at] = jnp.where(lower, c[j], up[j])
                for i in range(4):
                    field[i, 4 + at] = up[i]
                    field[10 + i, 4 + at] = down[i]
                if side == 0:
                    kept = c
            for i in range(6):
                zs[k, g, i, y] = jnp.where(cross, pltpu.roll(kept[i], 64, 1), c[i])
            return carry

        copies = halo(k, g)
        lax.fori_loop(0, 6, pack, 0, unroll=6)
        for cp in copies:
            cp.start()

    def receive(k, g):
        field = e.at[k, g]
        for cp in halo(k, g):
            cp.wait_recv()

        def unpack(y, carry):
            for j in range(2):
                before, after = xr[k, g, 0, j, y], xr[k, g, 1, j, y]
                field[j, 4 + y] = jnp.where(lower, before, field[j, 4 + y])
                field[2 + j, 4 + y] = jnp.where(lower, pltpu.roll(before, 96, 1), field[2 + j, 4 + y])
                field[10 + j, 4 + y] = jnp.where(lower, field[10 + j, 4 + y], pltpu.roll(after, 32, 1))
                field[12 + j, 4 + y] = jnp.where(lower, field[12 + j, 4 + y], after)
            return carry

        lax.fori_loop(0, 12, unpack, 0, unroll=12)

    def stencil(k, g):
        factor = 1.0 if k == 0 else 2.0
        factors = [-0.1 * factor * c for c in coef_list]
        field = e.at[k, g]

        def layer(i, carry):
            column = [field[i + 4, y] for y in range(20)]
            for y in range(12):
                c = column[y + 4]
                beyond = zr[k, g, i, y % 6]
                if y >= 6:
                    beyond = pltpu.roll(beyond, 64, 1)
                beyond = jnp.where(cross, beyond, pltpu.roll(c, 64, 1))
                total = factor * diag[i, y] * c
                for m in range(1, 5):
                    up = pltpu.roll(jnp.where(sub < m, beyond, c), 8 - m, 0)
                    down = pltpu.roll(jnp.where(sub >= 8 - m, beyond, c), m, 0)
                    near = ((up + down) + (column[y + 4 + m] + column[y + 4 - m])
                            + (field[i + 4 + m, y + 4] + field[i + 4 - m, y + 4]))
                    total = total + factors[m - 1] * near
                if k > 0:
                    total = total - e[k - 1, g, i + 4, y + 4]
                if k < 2:
                    e[k + 1, g, i + 4, y + 4] = total
                elif g == 0:
                    done[i, y] = total
                else:
                    even = jnp.where(lower, done[i, y], pltpu.roll(total, 32, 1))
                    odd = jnp.where(lower, pltpu.roll(done[i, y], 96, 1), total)
                    for xh, v in enumerate((even, odd)):
                        out_ref[i + 6 * xh, y, 0:8, :] = v[:, 0:64]
                        out_ref[i + 6 * xh, y, 8:16, :] = pltpu.roll(v, 64, 1)[:, 0:64]
            return carry

        lax.fori_loop(0, 6, layer, 0, unroll=2)

    for g in range(2):
        weights(g)
        acc = jnp.dot(ohi[...], w[g], preferred_element_type=jnp.float32)
        acc = acc + jnp.dot(olo[...], w[g], preferred_element_type=jnp.float32)
        e[0, g, pl.ds(4, 6), pl.ds(4, 12)] = (acc[:, 0:128] + acc[:, 128:256]).reshape(6, 12, 8, 128)
        send(0, g)

    for k in range(3):
        for g in range(2):
            receive(k, g)
            stencil(k, g)
            if k < 2:
                send(k + 1, g)

    for n, buf in enumerate((r1, r2, full)):
        all_arrived(n, buf).wait_send()
    for k in range(3):
        for g in range(2):
            for cp in halo(k, g):
                cp.wait_send()


def per_device(orbitals, potential, eig_blocks, owners, block_ids):
    hbm = pl.BlockSpec(memory_space=pl.ANY)
    f32, bf16 = jnp.float32, jnp.bfloat16
    scratch = [
        pltpu.SMEM((2,), jnp.int32),
        pltpu.SMEM((2,), jnp.int32),
        pltpu.VMEM((12, 12, 16), f32),
        pltpu.VMEM((12, 12, 16, 256), f32),
        pltpu.VMEM((256, 256), f32),
        pltpu.VMEM((16, 8, 128), f32),
        pltpu.VMEM((16, 8, 128), f32),
        pltpu.VMEM((16, 8, 128), f32),
        pltpu.VMEM((16, 8, 128), f32),
        pltpu.VMEM((3, 2, 14, 20, 8, 128), f32),
        pltpu.VMEM((6, 12, 8, 128), f32),
        pltpu.VMEM((3, 2, 2, 2, 12, 8, 128), f32),
        pltpu.VMEM((3, 2, 2, 2, 12, 8, 128), f32),
        pltpu.VMEM((3, 2, 6, 6, 8, 128), f32),
        pltpu.VMEM((3, 2, 6, 6, 8, 128), f32),
        pltpu.VMEM((6, 12, 8, 128), f32),
        pltpu.VMEM((576, 1024), bf16),
        pltpu.VMEM((576, 1024), bf16),
        pltpu.VMEM((2, 1024, 256), bf16),
        pltpu.SemaphoreType.DMA((5,)),
        pltpu.SemaphoreType.DMA((3,)),
        pltpu.SemaphoreType.DMA((3,)),
        pltpu.SemaphoreType.DMA((3, 2, 6)),
        pltpu.SemaphoreType.DMA((3, 2, 6)),
    ]
    return pl.pallas_call(
        kernel,
        out_shape=pltpu.VMEM((12, 12, 16, 64), f32),
        in_specs=[hbm] * 5,
        out_specs=pl.BlockSpec(memory_space=pltpu.VMEM),
        scratch_shapes=scratch,
        compiler_params=pltpu.CompilerParams(
            collective_id=0, has_side_effects=True, vmem_limit_bytes=56 * 2**20
        ),
        name="rotate_filter",
    )(owners, block_ids, orbitals, potential, eig_blocks)


def solution(mesh):
    placed = (P("gx", "gy", "gz", None), P("gx", "gy", "gz"), P(("gx", "gy", "gz"), None), P(), P())
    return jax.shard_map(
        per_device, mesh=mesh, in_specs=placed, out_specs=P("gx", "gy", "gz", None), check_vma=False
    )
```

```python
import jax
import jax.numpy as jnp
from jax import lax
from jax.experimental import pallas as pl
from jax.experimental.pallas import tpu as pltpu
from jax.sharding import PartitionSpec as P

MESH = pl.DeviceIdType.MESH
PCOL = 32
coef_list = (8.0 / 5.0, -1.0 / 5.0, 8.0 / 315.0, -1.0 / 560.0)
coef_zero = -205.0 / 72.0
center = 5.5
half = 5.0


def kernel(own_hbm, bid_hbm, orb_ref, pot_hbm, eig_ref, out_ref,
           own_ref, bid_ref, pot_ref, orb, eig, contrib, r1, r2, full, e, diag, xs, xr, zs, zr, done, ohi, olo, w,
           load_sem, g_send, g_recv, h_send, h_recv):
    gx, gy, gz = lax.axis_index("gx"), lax.axis_index("gy"), lax.axis_index("gz")
    x = lax.rem(gx, 4)
    zlo = lax.div(gx, 4)

    plane = []
    line = []
    for k in sorted(range(1, 16), key=lambda k: -min(k // 4, 4 - k // 4) - min(k % 4, 4 - k % 4)):
        px, py = lax.rem(x + k // 4, 4), lax.rem(gy + k % 4, 4)
        plane.append((k, px * 4 + py, (zlo * 4 + px, py, gz)))
    for k in sorted(range(1, 16), key=lambda k: -min(k % 8, 8 - k % 8)):
        pz, pc = lax.rem(zlo + k // 8, 2), lax.rem(gz + k % 8, 8)
        line.append((k, (pz * 4 + x, gy, pc)))
    me = x * 4 + gy
    xup, xdown = (lax.rem(gx + 1, 8), gy, gz), (lax.rem(gx + 7, 8), gy, gz)
    yup, ydown = (gx, lax.rem(gy + 1, 4), gz), (gx, lax.rem(gy + 3, 4), gz)
    zup, zdown = (gx, gy, lax.rem(gz + 1, 8)), (gx, gy, lax.rem(gz + 7, 8))

    barrier = pltpu.get_barrier_semaphore()
    peers = [p for _, _, p in plane] + [p for _, p in line]
    for p in peers[:15]:
        pl.semaphore_signal(barrier, inc=1, device_id=p, device_id_type=MESH)
    loads = [
        pltpu.make_async_copy(src, dst, load_sem.at[n])
        for n, (src, dst) in enumerate(((own_hbm, own_ref), (bid_hbm, bid_ref), (eig_ref, eig), (orb_ref, orb), (pot_hbm, pot_ref)))
    ]
    for n in range(3):
        loads[n].start()
    for p in peers[15:]:
        pl.semaphore_signal(barrier, inc=1, device_id=p, device_id_type=MESH)
    for n in range(3, 5):
        loads[n].start()

    for n in range(3):
        loads[n].wait()
    my_id = (gx * 4 + gy) * 8 + gz
    lane = lax.broadcasted_iota(jnp.int32, (256, 128), 1)
    row = lax.broadcasted_iota(jnp.int32, (256, 128), 0)
    state = lax.rem(lane, 64)
    first = state < PCOL
    owner = jnp.where(first, own_ref[0], own_ref[1])
    column = jnp.where(first, bid_ref[0], bid_ref[1]) * PCOL + lax.rem(state, PCOL)
    pick = jnp.where((row == column) & (owner == my_id), 1.0, 0.0)
    top = jnp.dot(eig[0:128], jnp.where(lane < 64, pick, 0.0), precision=lax.Precision.HIGHEST,
                  preferred_element_type=jnp.float32)
    low = jnp.dot(eig[128:256], jnp.where(lane < 64, 0.0, pick), precision=lax.Precision.HIGHEST,
                  preferred_element_type=jnp.float32)
    contrib[...] = (top + low).reshape(16, 8, 128)
    r1[0] = contrib[me]

    pl.semaphore_wait(barrier, len(peers))

    for k, j, dev in plane:
        pltpu.make_async_remote_copy(src_ref=contrib.at[j], dst_ref=r1.at[k], send_sem=g_send.at[0], recv_sem=g_recv.at[0],
                                     device_id=dev, device_id_type=MESH).start()

    def all_arrived(n, buf):
        return pltpu.make_async_remote_copy(src_ref=buf.at[pl.ds(1, 15)], dst_ref=buf.at[pl.ds(1, 15)], send_sem=g_send.at[n],
                                            recv_sem=g_recv.at[n], device_id=xup, device_id_type=MESH)

    all_arrived(0, r1).wait_recv()
    r2[0] = jnp.sum(r1[...], axis=0)
    for k, dev in line:
        pltpu.make_async_remote_copy(src_ref=r2.at[0], dst_ref=r2.at[k], send_sem=g_send.at[1], recv_sem=g_recv.at[1],
                                     device_id=dev, device_id_type=MESH).start()
    loads[3].wait()

    def split(i, carry):
        rows = pl.ds(pl.multiple_of(i * 96, 96), 96)
        for zh in range(2):
            for xh in range(2):
                o = orb[i + 6 * xh, :, pl.ds(8 * zh, 8), :].reshape(96, 256)
                hi = o.astype(jnp.bfloat16)
                columns = pl.ds(256 * (2 * zh + xh), 256)
                ohi[rows, columns] = hi
                olo[rows, columns] = (o - hi.astype(jnp.float32)).astype(jnp.bfloat16)
        return carry

    lax.fori_loop(0, 6, split, 0)

    all_arrived(1, r2).wait_recv()
    full[me] = jnp.sum(r2[...], axis=0)
    for k, j, dev in plane:
        pltpu.make_async_remote_copy(src_ref=full.at[me], dst_ref=full.at[me], send_sem=g_send.at[2], recv_sem=g_recv.at[2],
                                     device_id=dev, device_id_type=MESH).start()
    loads[4].wait()
    zmask = lax.broadcasted_iota(jnp.int32, (12, 8, 16), 1) == lax.rem(lax.broadcasted_iota(jnp.int32, (12, 8, 16), 2), 8)
    zhalf = lax.div(lax.broadcasted_iota(jnp.int32, (16, 128), 0), 8)
    quarter = lax.div(lax.broadcasted_iota(jnp.int32, (16, 128), 1), 32)

    def diagonal(i, carry):
        total = 0.0
        for xh in range(2):
            v = (pot_ref[i + 6 * xh] - center) / half - 0.3 * coef_zero
            a = jnp.where(zmask, jnp.broadcast_to(v[:, None, :], (12, 8, 16)), 0.0).reshape(96, 16)
            spread = jnp.where(quarter == 2 * zhalf + xh, 1.0, 0.0)
            total = total + jnp.dot(a, spread, precision=lax.Precision.HIGHEST, preferred_element_type=jnp.float32)
        diag[i] = total.reshape(12, 8, 128)
        return carry

    lax.fori_loop(0, 6, diagonal, 0)

    all_arrived(2, full).wait_recv()

    sub = lax.broadcasted_iota(jnp.int32, (8, 128), 0)
    lane = lax.broadcasted_iota(jnp.int32, (8, 128), 1)
    cross = (sub < 4) == (lane >= 64)
    lower = lax.rem(lane, 64) < 32
    wide = lax.div(lax.broadcasted_iota(jnp.int32, (128, 128), 1), 32)

    def weights(g):
        rot = full[...].reshape(128, 128)
        rolled = [rot] + [pltpu.roll(rot, 32 * r, 1) for r in range(1, 4)]
        for b in range(4):
            for kh in range(2):
                part = jnp.where(wide == b, rolled[(b - 2 * kh - g) % 4], 0.0)
                hi = part.astype(jnp.bfloat16)
                rows = pl.ds(256 * b + 128 * kh, 128)
                w[g, rows, 0:128] = hi
                w[g, rows, 128:256] = (part - hi.astype(jnp.float32)).astype(jnp.bfloat16)

    def halo(k, g):
        inner = pl.ds(4, 6)
        field = e.at[k, g]
        pairs = (
            (zs.at[k, g, :, :, pl.ds(4, 4)], zr.at[k, g, :, :, pl.ds(4, 4)], zup),
            (zs.at[k, g, :, :, pl.ds(0, 4)], zr.at[k, g, :, :, pl.ds(0, 4)], zdown),
            (xs.at[k, g, 0], xr.at[k, g, 0], xup),
            (xs.at[k, g, 1], xr.at[k, g, 1], xdown),
            (field.at[inner, pl.ds(12, 4)], field.at[inner, pl.ds(0, 4)], yup),
            (field.at[inner, pl.ds(4, 4)], field.at[inner, pl.ds(16, 4)], ydown),
        )
        return [
            pltpu.make_async_remote_copy(src_ref=src, dst_ref=dst, send_sem=h_send.at[k, g, n], recv_sem=h_recv.at[k, g, n],
                                         device_id=dev, device_id_type=MESH)
            for n, (src, dst, dev) in enumerate(pairs)
        ]

    def send(k, g):
        field = e.at[k, g]

        def pack(y, carry):
            for at, side in ((y, 0), (y + 6, 1)):
                c = [field[4 + i, 4 + at] for i in range(6)]
                up = [pltpu.roll(c[i], 32, 1) for i in range(2, 6)]
                down = [pltpu.roll(c[i], 96, 1) for i in range(4)]
                for j in range(2):
                    xs[k, g, 0, j, at] = jnp.where(lower, down[2 + j], c[4 + j])
                    xs[k, g, 1, j, at] = jnp.where(lower, c[j], up[j])
                for i in range(4):
                    field[i, 4 + at] = up[i]
                    field[10 + i, 4 + at] = down[i]
                if side == 0:
                    kept = c
            for i in range(6):
                zs[k, g, i, y] = jnp.where(cross, pltpu.roll(kept[i], 64, 1), c[i])
            return carry

        copies = halo(k, g)
        lax.fori_loop(0, 6, pack, 0, unroll=6)
        for cp in copies:
            cp.start()

    def receive(k, g):
        field = e.at[k, g]
        for cp in halo(k, g):
            cp.wait_recv()

        def unpack(y, carry):
            for j in range(2):
                before, after = xr[k, g, 0, j, y], xr[k, g, 1, j, y]
                field[j, 4 + y] = jnp.where(lower, before, field[j, 4 + y])
                field[2 + j, 4 + y] = jnp.where(lower, pltpu.roll(before, 96, 1), field[2 + j, 4 + y])
                field[10 + j, 4 + y] = jnp.where(lower, field[10 + j, 4 + y], pltpu.roll(after, 32, 1))
                field[12 + j, 4 + y] = jnp.where(lower, field[12 + j, 4 + y], after)
            return carry

        lax.fori_loop(0, 12, unpack, 0, unroll=12)

    def stencil(k, g):
        factor = 1.0 if k == 0 else 2.0
        factors = [-0.1 * factor * c for c in coef_list]
        field = e.at[k, g]

        def layer(i, carry):
            column = [field[i + 4, y] for y in range(20)]
            for y in range(12):
                c = column[y + 4]
                beyond = zr[k, g, i, y % 6]
                if y >= 6:
                    beyond = pltpu.roll(beyond, 64, 1)
                beyond = jnp.where(cross, beyond, pltpu.roll(c, 64, 1))
                total = factor * diag[i, y] * c
                for m in range(1, 5):
                    if m < 4:
                        up = pltpu.roll(jnp.where(sub < m, beyond, c), 8 - m, 0)
                        down = pltpu.roll(jnp.where(sub >= 8 - m, beyond, c), m, 0)
                        along = up + down
                    else:
                        along = pltpu.roll(beyond + c, 4, 0)
                    near = (along + (column[y + 4 + m] + column[y + 4 - m])
                            + (field[i + 4 + m, y + 4] + field[i + 4 - m, y + 4]))
                    total = total + factors[m - 1] * near
                if k > 0:
                    total = total - e[k - 1, g, i + 4, y + 4]
                if k < 2:
                    e[k + 1, g, i + 4, y + 4] = total
                elif g == 0:
                    done[i, y] = total
                else:
                    even = jnp.where(lower, done[i, y], pltpu.roll(total, 32, 1))
                    odd = jnp.where(lower, pltpu.roll(done[i, y], 96, 1), total)
                    for xh, v in enumerate((even, odd)):
                        out_ref[i + 6 * xh, y, 0:8, :] = v[:, 0:64]
                        out_ref[i + 6 * xh, y, 8:16, :] = pltpu.roll(v, 64, 1)[:, 0:64]
            return carry

        lax.fori_loop(0, 6, layer, 0, unroll=2)

    for g in range(2):
        weights(g)
        acc = jnp.dot(ohi[...], w[g], preferred_element_type=jnp.float32)
        acc = acc + jnp.dot(olo[...], w[g], preferred_element_type=jnp.float32)
        e[0, g, pl.ds(4, 6), pl.ds(4, 12)] = (acc[:, 0:128] + acc[:, 128:256]).reshape(6, 12, 8, 128)
        send(0, g)

    for n, buf in enumerate((r1, r2, full)):
        all_arrived(n, buf).wait_send()

    for k in range(3):
        for g in range(2):
            if k > 0:
                for cp in halo(k - 1, g):
                    cp.wait_send()
            if k == 2 and g == 1:
                for cp in halo(2, 0):
                    cp.wait_send()
            receive(k, g)
            stencil(k, g)
            if k < 2:
                send(k + 1, g)

    for cp in halo(2, 1):
        cp.wait_send()


def per_device(orbitals, potential, eig_blocks, owners, block_ids):
    hbm = pl.BlockSpec(memory_space=pl.ANY)
    f32, bf16 = jnp.float32, jnp.bfloat16
    scratch = [
        pltpu.SMEM((2,), jnp.int32),
        pltpu.SMEM((2,), jnp.int32),
        pltpu.VMEM((12, 12, 16), f32),
        pltpu.VMEM((12, 12, 16, 256), f32),
        pltpu.VMEM((256, 256), f32),
        pltpu.VMEM((16, 8, 128), f32),
        pltpu.VMEM((16, 8, 128), f32),
        pltpu.VMEM((16, 8, 128), f32),
        pltpu.VMEM((16, 8, 128), f32),
        pltpu.VMEM((3, 2, 14, 20, 8, 128), f32),
        pltpu.VMEM((6, 12, 8, 128), f32),
        pltpu.VMEM((3, 2, 2, 2, 12, 8, 128), f32),
        pltpu.VMEM((3, 2, 2, 2, 12, 8, 128), f32),
        pltpu.VMEM((3, 2, 6, 6, 8, 128), f32),
        pltpu.VMEM((3, 2, 6, 6, 8, 128), f32),
        pltpu.VMEM((6, 12, 8, 128), f32),
        pltpu.VMEM((576, 1024), bf16),
        pltpu.VMEM((576, 1024), bf16),
        pltpu.VMEM((2, 1024, 256), bf16),
        pltpu.SemaphoreType.DMA((5,)),
        pltpu.SemaphoreType.DMA((3,)),
        pltpu.SemaphoreType.DMA((3,)),
        pltpu.SemaphoreType.DMA((3, 2, 6)),
        pltpu.SemaphoreType.DMA((3, 2, 6)),
    ]
    return pl.pallas_call(
        kernel,
        out_shape=pltpu.VMEM((12, 12, 16, 64), f32),
        in_specs=[hbm] * 5,
        out_specs=pl.BlockSpec(memory_space=pltpu.VMEM),
        scratch_shapes=scratch,
        compiler_params=pltpu.CompilerParams(
            collective_id=0, has_side_effects=True, vmem_limit_bytes=56 * 2**20
        ),
        name="rotate_filter",
    )(owners, block_ids, orbitals, potential, eig_blocks)


def solution(mesh):
    placed = (P("gx", "gy", "gz", None), P("gx", "gy", "gz"), P(("gx", "gy", "gz"), None), P(), P())
    return jax.shard_map(
        per_device, mesh=mesh, in_specs=placed, out_specs=P("gx", "gy", "gz", None), check_vma=False
    )
```
